32 devices in a mesh: wide: 8 (over z, y), narrow: 4 (over x, core).
Axes of the slice: x: 2, y: 2, z: 4, core: 2. Of those that a mesh axis runs over, the one named last changes fastest.
Arguments:
- gradients: bfloat16 [32, 16, 1024], P(None, 'narrow', 'wide'), may hold values from -4000 to 4000
- offsets: int32 [16], P('narrow'), may hold values from 0 to 1048575
- seeds: int32 [2, 4096], replicated, may hold values from 1 to 8190
- inv_kernel: float32 [4096, 4096], P('wide', 'narrow'), may hold values from -2 to 2
- sketches: float32 [1024, 4096], P('wide', 'narrow'), may hold values from -6 to 6
Outputs:
- scores: float32 [32, 1024], P('narrow', 'wide')
The draws below stay inside these ranges and needn't reach their ends.
All inputs are finite; a program needn't handle non-finite values.
Results may differ from the reference program's by a relative error of at most 0.0023.
Values sent between devices are 32-bit elements; how exact they have to be, the bound alone decides.
A program may use at most 64 MiB of HBM per device.

```python
import math
import jax
import jax.numpy as jnp
from jax import lax

Q = 32
K = 4096
P_ROWS = 16
P_COLS = 1024
NTRAIN = 1024


def draw_gradients(key, part):
    first, second, third = jax.random.split(key, 3)
    row_scale = 10.0 ** jax.random.uniform(second, (Q, 1, 1), jnp.float32)
    col_pos = jnp.arange(P_COLS, dtype=jnp.float32) / P_COLS
    row_pos = jnp.arange(P_ROWS, dtype=jnp.float32) / P_ROWS
    trend = (10.0 ** col_pos)[None, :] * (3.0 ** row_pos)[:, None]
    rough = jnp.exp(jax.random.uniform(third, (Q, P_ROWS, P_COLS), jnp.float32, -0.35, 0.35))
    base = jnp.clip(jax.random.normal(first, (Q, P_ROWS, P_COLS), jnp.float32), -6.0, 6.0)
    return (base * rough * trend[None, :, :] * row_scale).astype(jnp.bfloat16)


def draw_inv_kernel(key, part):
    left = jnp.arange(K, dtype=jnp.int32)[:, None]
    right = jnp.arange(K, dtype=jnp.int32)[None, :]
    diagonal = (left == right).astype(jnp.float32)
    spread = jnp.clip(jax.random.normal(key, (K, K), jnp.float32), -6.0, 6.0)
    return diagonal + 0.6 * spread * K ** (-0.5)


def with_ends(result, own_key, smallest, top_value):
    place = [jax.random.randint(jax.random.fold_in(own_key, axis), (), 0, length) for axis, length in enumerate(result.shape)]
    longest = result.shape.index(max(result.shape))
    next_to = place[:longest] + [(place[longest] + 1) % result.shape[longest]] + place[longest + 1:]
    return result.at[tuple(place)].set(smallest).at[tuple(next_to)].set(top_value)


def block_scale(own_key, dims, shards, least, top_value):
    loudness = 1.0
    for axis_at, blocks in shards:
        heights = jax.random.uniform(jax.random.fold_in(jax.random.fold_in(own_key, 6), axis_at), (blocks,), jnp.float32, least / len(shards), top_value / len(shards))
        loudness = loudness * jnp.repeat(jnp.exp(heights), dims[axis_at] // blocks).reshape((-1,) + (1,) * (len(dims) - 1 - axis_at))
    return loudness


def noise(key, dims, scale, most, shards=(), kind=jnp.bfloat16):
    values = jax.random.normal(key, dims, jnp.float32) * scale
    if len(shards) > 0:
        values = block_scale(key, dims, shards, -0.22, 0.18) * values
    return jnp.clip(values, min=-most, max=most).astype(kind)


def setup_inputs(seed: int = 0) -> dict:
    streams_of = jax.random.split(jax.random.key(seed), 6)
    gradients = draw_gradients(jax.random.fold_in(streams_of[5], 71), 0)
    offsets = with_ends(jax.random.randint(streams_of[1], (P_ROWS,), 0, 1048576), jax.random.fold_in(streams_of[1], 1), 0, 1048575).astype(jnp.int32)
    seeds = with_ends(jax.random.randint(streams_of[2], (2, K), 1, 8191), jax.random.fold_in(streams_of[2], 1), 1, 8190).astype(jnp.int32)
    inv_kernel = draw_inv_kernel(jax.random.fold_in(streams_of[5], 71), 0)
    sketches = noise(streams_of[4], (NTRAIN, K), 1.0, 6.0, ((0, 8), (1, 4)), jnp.float32)
    return dict(gradients=gradients, offsets=offsets, seeds=seeds, inv_kernel=inv_kernel, sketches=sketches)


modulus = 8191
turn = 2.0 * math.pi / 8191.0
epsilon = 1e-06

def cosine_block(param_index, mults, adds):
    phase = ((param_index % modulus)[:, None] * (mults % modulus)[None, :] + adds[None, :]) % modulus
    return jnp.cos(phase.astype(jnp.float32) * turn).astype(jnp.bfloat16)

def reference(gradients, offsets, seeds, inv_kernel, sketches):
    queries, slab_rows, slab_cols = gradients.shape
    width = seeds.shape[1]
    step = min(width, 512)
    nblocks = width // step
    column_index = jnp.arange(slab_cols, dtype=jnp.int32)

    def one_row(carry, row):
        param_index = (offsets[row] + column_index).astype(jnp.int32)
        grad_row = lax.dynamic_index_in_dim(gradients, row, 1, keepdims=False)

        def one_block(block_id):
            start = (block_id * step).astype(jnp.int32)
            mults = lax.dynamic_slice_in_dim(seeds[0], start, step)
            adds = lax.dynamic_slice_in_dim(seeds[1], start, step)
            table = cosine_block(param_index, mults, adds)
            return jnp.dot(grad_row, table, preferred_element_type=jnp.float32)
        parts = lax.map(one_block, jnp.arange(nblocks, dtype=jnp.int32))
        return (carry + parts.transpose(1, 0, 2).reshape(queries, width), None)
    projected, _ = lax.scan(one_row, jnp.zeros((queries, width), jnp.float32), jnp.arange(slab_rows, dtype=jnp.int32))
    squares = lax.optimization_barrier(jnp.sum(jnp.square(gradients.astype(jnp.float32)), axis=(1, 2)))
    inverse_norm = 1.0 / jnp.sqrt(squares + epsilon)
    normalized = projected * inverse_norm[:, None]
    preconditioned = jnp.dot(normalized, inv_kernel, precision=lax.Precision.HIGHEST, preferred_element_type=jnp.float32)
    scores = lax.dot_general(preconditioned, sketches, (((1,), (1,)), ((), ())), precision=lax.Precision.HIGHEST, preferred_element_type=jnp.float32)
    return scores / jnp.sqrt(jnp.float32(width))
```

```python
import functools
import math

import jax
import jax.numpy as jnp
from jax import lax
from jax.experimental import pallas as pl
from jax.experimental.pallas import tpu as pltpu
from jax.sharding import PartitionSpec as P

modulus = 8191
turn = 2.0 * math.pi / 8191.0
epsilon = 1e-06


def cosine_block(param_index, mults, adds):
    phase = (
        (param_index % modulus)[:, None] * (mults % modulus)[None, :] + adds[None, :]
    ) % modulus
    return jnp.cos(phase.astype(jnp.float32) * turn).astype(jnp.bfloat16)


def body(gradients, offsets, seeds, inv_kernel, sketches):
    queries = gradients.shape[0]
    cols_dev = gradients.shape[2]
    flat_grad = gradients.reshape(queries, -1)
    width = seeds.shape[1]
    n_wide = lax.axis_size("wide")
    n_narrow = lax.axis_size("narrow")
    param_index = (
        offsets[:, None]
        + lax.axis_index("wide") * cols_dev
        + jnp.arange(cols_dev, dtype=jnp.int32)[None, :]
    ).reshape(-1)
    local_squares = jnp.sum(jnp.square(flat_grad.astype(jnp.float32)), axis=1)
    start = jnp.int32(0)
    step = min(lax.axis_size("wide") * (width // n_wide), 512)
    pieces = []
    for block_id in range(lax.axis_size("wide") * (width // n_wide) // step):
        begin = start + block_id * step
        mults = lax.dynamic_slice_in_dim(seeds[0], begin, step)
        adds = lax.dynamic_slice_in_dim(seeds[1], begin, step)
        table = cosine_block(param_index, mults, adds)
        term = jnp.einsum("pk,qp->kq", table, flat_grad, preferred_element_type=jnp.float32)
        pieces.append(term)
    owned = lax.psum_scatter(
        jnp.concatenate(pieces, axis=0), "wide", scatter_dimension=0, tiled=True
    )
    owned = lax.psum(owned, "narrow")
    kernel_part = lax.dot_general(
        owned,
        inv_kernel,
        (((0,), (0,)), ((), ())),
        precision=lax.Precision.HIGHEST,
        preferred_element_type=jnp.float32,
    )
    preconditioned = lax.psum(kernel_part, "wide")
    rows = queries // n_narrow
    root = jnp.sqrt(jnp.float32(width))
    product = lax.dot_general(
        preconditioned,
        sketches,
        (((1,), (1,)), ((), ())),
        precision=lax.Precision.HIGHEST,
        preferred_element_type=jnp.float32,
    )
    scores = lax.psum_scatter(product / root, "narrow", scatter_dimension=0, tiled=True)
    total = lax.psum(local_squares, ("wide", "narrow"))
    late_scale = 1.0 / jnp.sqrt(total + epsilon)
    mine = lax.dynamic_slice_in_dim(late_scale, lax.axis_index("narrow") * rows, rows)
    scores = scores * mine[:, None]
    return scores


def split(value):
    high = value.astype(jnp.bfloat16)
    low = (value - high.astype(jnp.float32)).astype(jnp.bfloat16)
    return high, low


def fold(value):
    return (value & modulus) + (value >> 13)


def cos_sin(phase):
    centred = jnp.where(phase > modulus // 2, phase - modulus, phase)
    half = centred.astype(jnp.float32) * jnp.float32(math.pi / modulus)
    square = half * half
    sine = jnp.full_like(square, -1.0 / math.factorial(11))
    for power in (9, 7, 5, 3, 1):
        sine = sine * square + jnp.float32((-1.0) ** (power // 2) / math.factorial(power))
    sine = sine * half
    cosine = jnp.full_like(square, 1.0 / math.factorial(12))
    for power in (10, 8, 6, 4, 2, 0):
        cosine = cosine * square + jnp.float32((-1.0) ** (power // 2) / math.factorial(power))
    return 1.0 - 2.0 * sine * sine, 2.0 * sine * cosine


def kernel(
    n_wide, n_narrow, grads_ref, offsets_ref, seeds_ref, inv_hbm, sketch_hbm, out_ref,
    inv_f32, sketch_f32, inv_hi, inv_lo, sketch_hi, sketch_lo,
    part, from_core, to_x, from_x, mine, from_wide, owned,
    product, from_wide2, full, scored, from_narrow,
    sq_mine, sq_narrow, sq_sum, sq_wide,
    local_sem, core_send, core_recv, x_send, x_recv, wide_send, wide_recv,
    gather_send, gather_recv, wide2_send, wide2_recv, full_send, full_recv,
    last_send, last_recv, sqn_send, sqn_recv, sqw_send, sqw_recv,
):
    w = lax.axis_index("wide")
    n = lax.axis_index("narrow")
    sibling = n + 1 - 2 * lax.rem(n, 2)
    across = lax.rem(n + 2, n_narrow)
    diagonal = lax.rem(sibling + 2, n_narrow)
    width = seeds_ref.shape[1]
    block = width // n_wide
    rows = offsets_ref.shape[0]
    cols = grads_ref.shape[1] // 2
    queries = grads_ref.shape[0] // rows

    def wide_peer(s):
        return lax.rem(w + s, n_wide)

    def narrow_peer(s):
        return lax.rem(n + s, n_narrow)

    def remote(src, dst, send, recv, to_wide, to_narrow):
        return pltpu.make_async_remote_copy(
            src_ref=src, dst_ref=dst, send_sem=send, recv_sem=recv,
            device_id=(to_wide, to_narrow), device_id_type=pl.DeviceIdType.MESH,
        )

    load_inv = pltpu.make_async_copy(inv_hbm, inv_f32, local_sem.at[0])
    load_sketch = pltpu.make_async_copy(sketch_hbm, sketch_f32, local_sem.at[1])
    load_inv.start()
    load_sketch.start()

    barrier = pltpu.get_barrier_semaphore()
    for s in range(1, n_wide):
        pl.semaphore_signal(barrier, inc=1, device_id=(wide_peer(s), n), device_id_type=pl.DeviceIdType.MESH)
    for s in range(1, n_narrow):
        pl.semaphore_signal(barrier, inc=1, device_id=(w, narrow_peer(s)), device_id_type=pl.DeviceIdType.MESH)

    grads = grads_ref[...]
    squares = jnp.square(grads[:, :cols].astype(jnp.float32))
    by_query = squares[:queries]
    for r in range(1, rows):
        by_query = by_query + squares[r * queries : (r + 1) * queries]
    by_query = jnp.broadcast_to(jnp.sum(by_query, axis=1, keepdims=True), (queries, 128))
    mine_rows = queries // n_narrow
    group = lax.broadcasted_iota(jnp.int32, (mine_rows, 128), 1) // (128 // n_narrow)
    tile = by_query[:mine_rows]
    for j in range(1, n_narrow):
        tile = jnp.where(group == j, by_query[j * mine_rows : (j + 1) * mine_rows], tile)
    sq_mine[...] = tile

    bases = [fold(offsets_ref[r] + w * cols) for r in range(rows)]
    steps = cols // 16

    def project(slab):
        def chunk(j, carry):
            units = []
            for half in range(2):
                start = pl.multiple_of((2 * j + half) * block + slab * 128, 128)
                units.append(seeds_ref[:, pl.ds(start, 128)])
            seeds = jnp.concatenate(units, axis=1)
            mult = fold(seeds[0:1])
            add = seeds[1:2]
            at = lax.broadcasted_iota(jnp.int32, (steps + 16, 256), 0)
            factor = jnp.where(at < steps, at * 16, at - steps)
            col_cos, col_sin = cos_sin(fold(fold(factor * mult)))
            at = lax.broadcasted_iota(jnp.int32, (8, 256), 0)
            base = jnp.full((8, 256), bases[0], jnp.int32)
            for r in range(1, rows):
                base = jnp.where(at == r, bases[r], base)
            row_cos, row_sin = cos_sin(fold(fold(base * mult + add)))
            low_cos, low_sin = col_cos[steps:], col_sin[steps:]
            cos_parts, sin_parts = [], []
            for h in range(steps):
                high_cos, high_sin = col_cos[h : h + 1], col_sin[h : h + 1]
                cos_parts.append(split(high_cos * low_cos - high_sin * low_sin))
                sin_parts.append(split(high_sin * low_cos + high_cos * low_sin))
            cos_table = jnp.concatenate([p[0] for p in cos_parts] + [p[1] for p in cos_parts], axis=0)
            sin_table = jnp.concatenate([p[0] for p in sin_parts] + [p[1] for p in sin_parts], axis=0)
            by_cos = jnp.dot(grads_ref[...], cos_table, preferred_element_type=jnp.float32)
            by_sin = jnp.dot(grads_ref[...], sin_table, preferred_element_type=jnp.float32)
            total = jnp.zeros((queries, 256), jnp.float32)
            for r in range(rows):
                here = slice(r * queries, (r + 1) * queries)
                total = total + (row_cos[r : r + 1] * by_cos[here] - row_sin[r : r + 1] * by_sin[here])
            part[slab, 2 * j] = total[:, :128]
            part[slab, 2 * j + 1] = total[:, 128:]
            return carry

        lax.fori_loop(0, n_wide // 2, chunk, 0)

    project(diagonal)
    pl.semaphore_wait(barrier, n_wide + n_narrow - 2)
    core_copies = []
    copy = remote(part.at[diagonal], from_core.at[0], core_send.at[0], core_recv.at[0], w, sibling)
    copy.start()
    core_copies.append(copy)
    sqn_copies = []
    for s in range(1, n_narrow):
        copy = remote(sq_mine, sq_narrow.at[s - 1], sqn_send.at[s - 1], sqn_recv.at[s - 1], w, narrow_peer(s))
        copy.start()
        sqn_copies.append(copy)
    project(sibling)
    copy = remote(part.at[sibling], from_core.at[1], core_send.at[1], core_recv.at[1], w, sibling)
    copy.start()
    core_copies.append(copy)
    project(across)
    core_copies[0].wait_recv()
    order = [*range(1, n_wide), 0]
    x_copies = []
    for s in order:
        at = wide_peer(s)
        to_x[at] = part[across, at] + from_core[0, at]
        copy = remote(to_x.at[at], from_x.at[at], x_send.at[s], x_recv.at[s], w, across)
        copy.start()
        x_copies.append(copy)
    project(n)
    core_copies[1].wait_recv()
    wide_copies = []
    for s, x_copy in zip(order, x_copies):
        at = wide_peer(s)
        x_copy.wait_recv()
        mine[at] = part[n, at] + from_core[1, at] + from_x[at]
        if s:
            copy = remote(mine.at[at], from_wide.at[s - 1], wide_send.at[s - 1], wide_recv.at[s - 1], at, n)
            copy.start()
            wide_copies.append(copy)
    for copy in sqn_copies:
        copy.wait_recv()
    total = sq_mine[...]
    for s in range(1, n_narrow):
        total = total + sq_narrow[s - 1]
    sq_sum[...] = total
    sqw_copies = []
    for s in range(1, n_wide):
        copy = remote(sq_sum, sq_wide.at[s - 1], sqw_send.at[s - 1], sqw_recv.at[s - 1], wide_peer(s), n)
        copy.start()
        sqw_copies.append(copy)
    load_inv.wait()
    load_sketch.wait()
    slab_rows = 32

    def split_inv(i, carry):
        at = pl.ds(pl.multiple_of(i * slab_rows, slab_rows), slab_rows)
        inv_hi[at, :], inv_lo[at, :] = split(inv_f32[at, :])
        return carry

    def split_sketch(i, carry):
        at = pl.ds(pl.multiple_of(i * slab_rows, slab_rows), slab_rows)
        sketch_hi[at, :], sketch_lo[at, :] = split(sketch_f32[at, :])
        return carry

    lax.fori_loop(0, inv_f32.shape[0] // slab_rows, split_inv, 0)
    lax.fori_loop(0, sketch_f32.shape[0] // slab_rows, split_sketch, 0)

    total = mine[w]
    for s in range(1, n_wide):
        wide_copies[s - 1].wait_recv()
        total = total + from_wide[s - 1]
    owned[n] = total
    gather_copies = []
    for s in range(1, n_narrow):
        copy = remote(owned.at[n], owned.at[n], gather_send.at[s - 1], gather_recv.at[s - 1], w, narrow_peer(s))
        copy.start()
        gather_copies.append(copy)
    for copy in gather_copies:
        copy.wait_recv()
    high, low = split(jnp.concatenate([owned[i] for i in range(n_narrow)], axis=1))
    both = jnp.dot(jnp.concatenate([high, low], axis=0), inv_hi[...], preferred_element_type=jnp.float32)
    both = both[:queries] + both[queries:] + jnp.dot(high, inv_lo[...], preferred_element_type=jnp.float32)
    for i in range(n_wide):
        product[i] = both[:, i * 128 : (i + 1) * 128]
    wide2_copies = []
    for s in range(1, n_wide):
        at = wide_peer(s)
        copy = remote(product.at[at], from_wide2.at[s - 1], wide2_send.at[s - 1], wide2_recv.at[s - 1], at, n)
        copy.start()
        wide2_copies.append(copy)
    total = sq_sum[...]
    for s in range(1, n_wide):
        sqw_copies[s - 1].wait_recv()
        total = total + sq_wide[s - 1]
    own_squares = jnp.max(jnp.where(group == n, total, 0.0), axis=1, keepdims=True)
    scale = 1.0 / jnp.sqrt(own_squares + epsilon)
    scale = scale * jnp.float32(1.0 / math.sqrt(width))

    total = product[w]
    for s in range(1, n_wide):
        wide2_copies[s - 1].wait_recv()
        total = total + from_wide2[s - 1]
    full[w] = total
    full_copies = []
    for s in range(1, n_wide):
        copy = remote(full.at[w], full.at[w], full_send.at[s - 1], full_recv.at[s - 1], wide_peer(s), n)
        copy.start()
        full_copies.append(copy)
    for copy in full_copies:
        copy.wait_recv()
    high, low = split(jnp.concatenate([full[i] for i in range(n_wide)], axis=1))
    last = (((1,), (1,)), ((), ()))
    both = lax.dot_general(jnp.concatenate([high, low], axis=0), sketch_hi[...], last, preferred_element_type=jnp.float32)
    both = both[:queries] + both[queries:] + lax.dot_general(
        high, sketch_lo[...], last, preferred_element_type=jnp.float32
    )
    for i in range(n_narrow):
        scored[i] = both[i * mine_rows : (i + 1) * mine_rows]
    last_copies = []
    for s in range(1, n_narrow):
        at = narrow_peer(s)
        copy = remote(scored.at[at], from_narrow.at[s - 1], last_send.at[s - 1], last_recv.at[s - 1], w, at)
        copy.start()
        last_copies.append(copy)
    total = scored[n]
    for s in range(1, n_narrow):
        last_copies[s - 1].wait_recv()
        total = total + from_narrow[s - 1]
    out_ref[...] = total * scale
    for group_copies in (
        core_copies, x_copies, wide_copies, sqn_copies, sqw_copies, gather_copies, wide2_copies, full_copies, last_copies,
    ):
        for copy in group_copies:
            copy.wait_send()


def fused(n_wide, n_narrow, gradients, offsets, seeds, inv_kernel, sketches):
    queries, rows, cols = gradients.shape
    width = seeds.shape[1]
    depth, span = inv_kernel.shape
    trains = sketches.shape[0]
    grads = gradients.transpose(1, 0, 2).reshape(rows * queries, cols)
    grads = jnp.concatenate([grads, grads], axis=1)
    unit = (queries, 128)
    mine_rows = queries // n_narrow
    f32, bf16 = jnp.float32, jnp.bfloat16

    def sems(count):
        return [pltpu.SemaphoreType.DMA((count,))] * 2

    vmem = pl.BlockSpec(memory_space=pltpu.VMEM)
    return pl.pallas_call(
        functools.partial(kernel, n_wide, n_narrow),
        out_shape=jax.ShapeDtypeStruct((mine_rows, trains), f32),
        in_specs=[
            vmem,
            pl.BlockSpec(memory_space=pltpu.SMEM),
            vmem,
            pl.BlockSpec(memory_space=pl.ANY),
            pl.BlockSpec(memory_space=pl.ANY),
        ],
        out_specs=vmem,
        scratch_shapes=[
            pltpu.VMEM((depth, span), f32),
            pltpu.VMEM((trains, span), f32),
            pltpu.VMEM((depth, span), bf16),
            pltpu.VMEM((depth, span), bf16),
            pltpu.VMEM((trains, span), bf16),
            pltpu.VMEM((trains, span), bf16),
            pltpu.VMEM((n_narrow, n_wide) + unit, f32),
            pltpu.VMEM((2, n_wide) + unit, f32),
            pltpu.VMEM((n_wide,) + unit, f32),
            pltpu.VMEM((n_wide,) + unit, f32),
            pltpu.VMEM((n_wide,) + unit, f32),
            pltpu.VMEM((n_wide - 1,) + unit, f32),
            pltpu.VMEM((n_narrow,) + unit, f32),
            pltpu.VMEM((n_wide,) + unit, f32),
            pltpu.VMEM((n_wide - 1,) + unit, f32),
            pltpu.VMEM((n_wide,) + unit, f32),
            pltpu.VMEM((n_narrow, mine_rows, trains), f32),
            pltpu.VMEM((n_narrow - 1, mine_rows, trains), f32),
            pltpu.VMEM((mine_rows, 128), f32),
            pltpu.VMEM((n_narrow - 1, mine_rows, 128), f32),
            pltpu.VMEM((mine_rows, 128), f32),
            pltpu.VMEM((n_wide - 1, mine_rows, 128), f32),
            pltpu.SemaphoreType.DMA((2,)),
            *sems(2),
            *sems(n_wide),
            *sems(n_wide - 1),
            *sems(n_narrow - 1),
            *sems(n_wide - 1),
            *sems(n_wide - 1),
            *sems(n_narrow - 1),
            *sems(n_narrow - 1),
            *sems(n_wide - 1),
        ],
        compiler_params=pltpu.CompilerParams(
            collective_id=0, has_side_effects=True, vmem_limit_bytes=32 * 1024 * 1024
        ),
    )(grads, offsets, seeds, inv_kernel, sketches)


def solution(mesh):
    placed = (P(None, "narrow", "wide"), P("narrow"), P(), P("wide", "narrow"), P("wide", "narrow"))
    n_wide, n_narrow = mesh.shape["wide"], mesh.shape["narrow"]

    def local(gradients, offsets, seeds, inv_kernel, sketches):
        queries, rows, cols = gradients.shape
        fits = (
            seeds.shape[1] == n_wide * n_narrow * 128
            and n_narrow == 4
            and n_wide % 2 == 0
            and cols == 128
            and rows <= 8
            and queries % (8 * n_narrow) == 0
            and sketches.shape[0] == 128
        )
        if fits:
            return fused(n_wide, n_narrow, gradients, offsets, seeds, inv_kernel, sketches)
        return body(gradients, offsets, seeds, inv_kernel, sketches)

    return jax.shard_map(
        local, mesh=mesh, in_specs=placed, out_specs=P("narrow", "wide"), check_vma=False
    )
```

```python
import functools
import math

import jax
import jax.numpy as jnp
from jax import lax
from jax.experimental import pallas as pl
from jax.experimental.pallas import tpu as pltpu
from jax.sharding import PartitionSpec as P

modulus = 8191
turn = 2.0 * math.pi / 8191.0
epsilon = 1e-06


def cosine_block(param_index, mults, adds):
    phase = (
        (param_index % modulus)[:, None] * (mults % modulus)[None, :] + adds[None, :]
    ) % modulus
    return jnp.cos(phase.astype(jnp.float32) * turn).astype(jnp.bfloat16)


def body(gradients, offsets, seeds, inv_kernel, sketches):
    queries = gradients.shape[0]
    cols_dev = gradients.shape[2]
    flat_grad = gradients.reshape(queries, -1)
    width = seeds.shape[1]
    n_wide = lax.axis_size("wide")
    n_narrow = lax.axis_size("narrow")
    param_index = (
        offsets[:, None]
        + lax.axis_index("wide") * cols_dev
        + jnp.arange(cols_dev, dtype=jnp.int32)[None, :]
    ).reshape(-1)
    local_squares = jnp.sum(jnp.square(flat_grad.astype(jnp.float32)), axis=1)
    start = jnp.int32(0)
    step = min(lax.axis_size("wide") * (width // n_wide), 512)
    pieces = []
    for block_id in range(lax.axis_size("wide") * (width // n_wide) // step):
        begin = start + block_id * step
        mults = lax.dynamic_slice_in_dim(seeds[0], begin, step)
        adds = lax.dynamic_slice_in_dim(seeds[1], begin, step)
        table = cosine_block(param_index, mults, adds)
        term = jnp.einsum("pk,qp->kq", table, flat_grad, preferred_element_type=jnp.float32)
        pieces.append(term)
    owned = lax.psum_scatter(
        jnp.concatenate(pieces, axis=0), "wide", scatter_dimension=0, tiled=True
    )
    owned = lax.psum(owned, "narrow")
    kernel_part = lax.dot_general(
        owned,
        inv_kernel,
        (((0,), (0,)), ((), ())),
        precision=lax.Precision.HIGHEST,
        preferred_element_type=jnp.float32,
    )
    preconditioned = lax.psum(kernel_part, "wide")
    rows = queries // n_narrow
    root = jnp.sqrt(jnp.float32(width))
    product = lax.dot_general(
        preconditioned,
        sketches,
        (((1,), (1,)), ((), ())),
        precision=lax.Precision.HIGHEST,
        preferred_element_type=jnp.float32,
    )
    scores = lax.psum_scatter(product / root, "narrow", scatter_dimension=0, tiled=True)
    total = lax.psum(local_squares, ("wide", "narrow"))
    late_scale = 1.0 / jnp.sqrt(total + epsilon)
    mine = lax.dynamic_slice_in_dim(late_scale, lax.axis_index("narrow") * rows, rows)
    scores = scores * mine[:, None]
    return scores


def split(value):
    high = value.astype(jnp.bfloat16)
    low = (value - high.astype(jnp.float32)).astype(jnp.bfloat16)
    return high, low


def fold(value):
    return (value & modulus) + (value >> 13)


def cos_sin(phase):
    centred = jnp.where(phase > modulus // 2, phase - modulus, phase)
    half = centred.astype(jnp.float32) * jnp.float32(math.pi / modulus)
    square = half * half
    sine = jnp.full_like(square, -1.0 / math.factorial(11))
    for power in (9, 7, 5, 3, 1):
        sine = sine * square + jnp.float32((-1.0) ** (power // 2) / math.factorial(power))
    sine = sine * half
    cosine = jnp.full_like(square, 1.0 / math.factorial(12))
    for power in (10, 8, 6, 4, 2, 0):
        cosine = cosine * square + jnp.float32((-1.0) ** (power // 2) / math.factorial(power))
    return 1.0 - 2.0 * sine * sine, 2.0 * sine * cosine


def kernel(
    n_wide, n_narrow, grads_hbm, offsets_hbm, seeds_hbm, inv_hbm, sketch_hbm, out_ref,
    grads_in, grads_f32, grads_ref, offsets_ref, seeds_ref, inv_f32, sketch_f32, inv_hi, inv_lo, sketch_hi, sketch_lo,
    part, from_core, to_x, from_x, mine, from_wide, owned,
    product, from_wide2, full, scored, from_narrow,
    sq_mine, sq_narrow, sq_sum, sq_wide,
    local_sem, core_send, core_recv, x_send, x_recv, wide_send, wide_recv,
    gather_send, gather_recv, wide2_send, wide2_recv, full_send, full_recv,
    last_send, last_recv, sqn_send, sqn_recv, sqw_send, sqw_recv,
):
    w = lax.axis_index("wide")
    n = lax.axis_index("narrow")
    sibling = n + 1 - 2 * lax.rem(n, 2)
    across = lax.rem(n + 2, n_narrow)
    diagonal = lax.rem(sibling + 2, n_narrow)
    width = seeds_ref.shape[1]
    block = width // n_wide
    rows = offsets_ref.shape[0]
    queries, _, cols = grads_in.shape

    def wide_peer(s):
        return lax.rem(w + s, n_wide)

    def narrow_peer(s):
        return lax.rem(n + s, n_narrow)

    def remote(src, dst, send, recv, to_wide, to_narrow):
        return pltpu.make_async_remote_copy(
            src_ref=src, dst_ref=dst, send_sem=send, recv_sem=recv,
            device_id=(to_wide, to_narrow), device_id_type=pl.DeviceIdType.MESH,
        )

    load_inv = pltpu.make_async_copy(inv_hbm, inv_f32, local_sem.at[0])
    load_sketch = pltpu.make_async_copy(sketch_hbm, sketch_f32, local_sem.at[1])
    load_grads = pltpu.make_async_copy(grads_hbm, grads_in, local_sem.at[2])
    load_seeds = pltpu.make_async_copy(seeds_hbm, seeds_ref, local_sem.at[3])
    load_offsets = pltpu.make_async_copy(offsets_hbm, offsets_ref, local_sem.at[4])
    load_grads.start()
    load_seeds.start()
    load_offsets.start()
    load_inv.start()
    load_sketch.start()

    barrier = pltpu.get_barrier_semaphore()
    for s in range(1, n_wide):
        pl.semaphore_signal(barrier, inc=1, device_id=(wide_peer(s), n), device_id_type=pl.DeviceIdType.MESH)
    for s in range(1, n_narrow):
        pl.semaphore_signal(barrier, inc=1, device_id=(w, narrow_peer(s)), device_id_type=pl.DeviceIdType.MESH)

    load_grads.wait()
    grads_f32[...] = grads_in[...].astype(jnp.float32)
    by_query = jnp.zeros((queries, cols), jnp.float32)
    for r in range(rows):
        one_row = grads_f32[:, r, :]
        by_query = by_query + jnp.square(one_row)
        one_row = one_row.astype(jnp.bfloat16)
        grads_ref[r * queries : (r + 1) * queries, :cols] = one_row
        grads_ref[r * queries : (r + 1) * queries, cols:] = one_row
    by_query = jnp.broadcast_to(jnp.sum(by_query, axis=1, keepdims=True), (queries, 128))
    mine_rows = queries // n_narrow
    group = lax.broadcasted_iota(jnp.int32, (mine_rows, 128), 1) // (128 // n_narrow)
    tile = by_query[:mine_rows]
    for j in range(1, n_narrow):
        tile = jnp.where(group == j, by_query[j * mine_rows : (j + 1) * mine_rows], tile)
    sq_mine[...] = tile

    load_offsets.wait()
    load_seeds.wait()
    bases = [fold(offsets_ref[r] + w * cols) for r in range(rows)]
    steps = cols // 16

    def project(slab):
        def chunk(j, carry):
            units = []
            for half in range(2):
                start = pl.multiple_of((2 * j + half) * block + slab * 128, 128)
                units.append(seeds_ref[:, pl.ds(start, 128)])
            seeds = jnp.concatenate(units, axis=1)
            mult = fold(seeds[0:1])
            add = seeds[1:2]
            at = lax.broadcasted_iota(jnp.int32, (steps + 16, 256), 0)
            factor = jnp.where(at < steps, at * 16, at - steps)
            col_cos, col_sin = cos_sin(fold(fold(factor * mult)))
            at = lax.broadcasted_iota(jnp.int32, (8, 256), 0)
            base = jnp.full((8, 256), bases[0], jnp.int32)
            for r in range(1, rows):
                base = jnp.where(at == r, bases[r], base)
            row_cos, row_sin = cos_sin(fold(fold(base * mult + add)))
            low_cos, low_sin = col_cos[steps:], col_sin[steps:]
            cos_parts, sin_parts = [], []
            for h in range(steps):
                high_cos, high_sin = col_cos[h : h + 1], col_sin[h : h + 1]
                cos_parts.append(split(high_cos * low_cos - high_sin * low_sin))
                sin_parts.append(split(high_sin * low_cos + high_cos * low_sin))
            cos_table = jnp.concatenate([p[0] for p in cos_parts] + [p[1] for p in cos_parts], axis=0)
            sin_table = jnp.concatenate([p[0] for p in sin_parts] + [p[1] for p in sin_parts], axis=0)
            by_cos = jnp.dot(grads_ref[...], cos_table, preferred_element_type=jnp.float32)
            by_sin = jnp.dot(grads_ref[...], sin_table, preferred_element_type=jnp.float32)
            total = jnp.zeros((queries, 256), jnp.float32)
            for r in range(rows):
                here = slice(r * queries, (r + 1) * queries)
                total = total + (row_cos[r : r + 1] * by_cos[here] - row_sin[r : r + 1] * by_sin[here])
            part[slab, 2 * j] = total[:, :128]
            part[slab, 2 * j + 1] = total[:, 128:]
            return carry

        lax.fori_loop(0, n_wide // 2, chunk, 0)

    project(diagonal)
    pl.semaphore_wait(barrier, n_wide + n_narrow - 2)
    core_copies = []
    copy = remote(part.at[diagonal], from_core.at[0], core_send.at[0], core_recv.at[0], w, sibling)
    copy.start()
    core_copies.append(copy)
    sqn_copies = []
    for s in range(1, n_narrow):
        copy = remote(sq_mine, sq_narrow.at[s - 1], sqn_send.at[s - 1], sqn_recv.at[s - 1], w, narrow_peer(s))
        copy.start()
        sqn_copies.append(copy)
    project(sibling)
    copy = remote(part.at[sibling], from_core.at[1], core_send.at[1], core_recv.at[1], w, sibling)
    copy.start()
    core_copies.append(copy)
    project(across)
    core_copies[0].wait_recv()
    order = [*range(1, n_wide), 0]
    x_copies = []
    for s in order:
        at = wide_peer(s)
        to_x[at] = part[across, at] + from_core[0, at]
        copy = remote(to_x.at[at], from_x.at[at], x_send.at[s], x_recv.at[s], w, across)
        copy.start()
        x_copies.append(copy)
    project(n)
    core_copies[1].wait_recv()
    wide_copies = []
    for s, x_copy in zip(order, x_copies):
        at = wide_peer(s)
        x_copy.wait_recv()
        mine[at] = part[n, at] + from_core[1, at] + from_x[at]
        if s:
            copy = remote(mine.at[at], from_wide.at[s - 1], wide_send.at[s - 1], wide_recv.at[s - 1], at, n)
            copy.start()
            wide_copies.append(copy)
    for copy in sqn_copies:
        copy.wait_recv()
    total = sq_mine[...]
    for s in range(1, n_narrow):
        total = total + sq_narrow[s - 1]
    sq_sum[...] = total
    sqw_copies = []
    for s in range(1, n_wide):
        copy = remote(sq_sum, sq_wide.at[s - 1], sqw_send.at[s - 1], sqw_recv.at[s - 1], wide_peer(s), n)
        copy.start()
        sqw_copies.append(copy)
    load_inv.wait()
    load_sketch.wait()
    slab_rows = 32

    def split_inv(i, carry):
        at = pl.ds(pl.multiple_of(i * slab_rows, slab_rows), slab_rows)
        inv_hi[at, :], inv_lo[at, :] = split(inv_f32[at, :])
        return carry

    def split_sketch(i, carry):
        at = pl.ds(pl.multiple_of(i * slab_rows, slab_rows), slab_rows)
        sketch_hi[at, :], sketch_lo[at, :] = split(sketch_f32[at, :])
        return carry

    lax.fori_loop(0, inv_f32.shape[0] // slab_rows, split_inv, 0)
    lax.fori_loop(0, sketch_f32.shape[0] // slab_rows, split_sketch, 0)

    total = mine[w]
    for s in range(1, n_wide):
        wide_copies[s - 1].wait_recv()
        total = total + from_wide[s - 1]
    owned[n] = total
    gather_copies = []
    for s in range(1, n_narrow):
        copy = remote(owned.at[n], owned.at[n], gather_send.at[s - 1], gather_recv.at[s - 1], w, narrow_peer(s))
        copy.start()
        gather_copies.append(copy)
    for copy in gather_copies:
        copy.wait_recv()
    high, low = split(jnp.concatenate([owned[i] for i in range(n_narrow)], axis=1))
    both = jnp.dot(jnp.concatenate([high, low], axis=0), inv_hi[...], preferred_element_type=jnp.float32)
    both = both[:queries] + both[queries:] + jnp.dot(high, inv_lo[...], preferred_element_type=jnp.float32)
    for i in range(n_wide):
        product[i] = both[:, i * 128 : (i + 1) * 128]
    wide2_copies = []
    for s in range(1, n_wide):
        at = wide_peer(s)
        copy = remote(product.at[at], from_wide2.at[s - 1], wide2_send.at[s - 1], wide2_recv.at[s - 1], at, n)
        copy.start()
        wide2_copies.append(copy)
    total = sq_sum[...]
    for s in range(1, n_wide):
        sqw_copies[s - 1].wait_recv()
        total = total + sq_wide[s - 1]
    own_squares = jnp.max(jnp.where(group == n, total, 0.0), axis=1, keepdims=True)
    scale = 1.0 / jnp.sqrt(own_squares + epsilon)
    scale = scale * jnp.float32(1.0 / math.sqrt(width))

    total = product[w]
    for s in range(1, n_wide):
        wide2_copies[s - 1].wait_recv()
        total = total + from_wide2[s - 1]
    full[w] = total
    full_copies = []
    for s in range(1, n_wide):
        copy = remote(full.at[w], full.at[w], full_send.at[s - 1], full_recv.at[s - 1], wide_peer(s), n)
        copy.start()
        full_copies.append(copy)
    for copy in full_copies:
        copy.wait_recv()
    high, low = split(jnp.concatenate([full[i] for i in range(n_wide)], axis=1))
    last = (((1,), (1,)), ((), ()))
    both = lax.dot_general(jnp.concatenate([high, low], axis=0), sketch_hi[...], last, preferred_element_type=jnp.float32)
    both = both[:queries] + both[queries:] + lax.dot_general(
        high, sketch_lo[...], last, preferred_element_type=jnp.float32
    )
    for i in range(n_narrow):
        scored[i] = both[i * mine_rows : (i + 1) * mine_rows]
    last_copies = []
    for s in range(1, n_narrow):
        at = narrow_peer(s)
        copy = remote(scored.at[at], from_narrow.at[s - 1], last_send.at[s - 1], last_recv.at[s - 1], w, at)
        copy.start()
        last_copies.append(copy)
    total = scored[n]
    for s in range(1, n_narrow):
        last_copies[s - 1].wait_recv()
        total = total + from_narrow[s - 1]
    out_ref[...] = total * scale
    for group_copies in (
        core_copies, x_copies, wide_copies, sqn_copies, sqw_copies, gather_copies, wide2_copies, full_copies, last_copies,
    ):
        for copy in group_copies:
            copy.wait_send()


def fused(n_wide, n_narrow, gradients, offsets, seeds, inv_kernel, sketches):
    queries, rows, cols = gradients.shape
    width = seeds.shape[1]
    depth, span = inv_kernel.shape
    trains = sketches.shape[0]
    unit = (queries, 128)
    mine_rows = queries // n_narrow
    f32, bf16 = jnp.float32, jnp.bfloat16

    def sems(count):
        return [pltpu.SemaphoreType.DMA((count,))] * 2

    return pl.pallas_call(
        functools.partial(kernel, n_wide, n_narrow),
        out_shape=jax.ShapeDtypeStruct((mine_rows, trains), f32),
        in_specs=[pl.BlockSpec(memory_space=pltpu.HBM)] * 5,
        out_specs=pl.BlockSpec(memory_space=pltpu.VMEM),
        scratch_shapes=[
            pltpu.VMEM((queries, rows, cols), bf16),
            pltpu.VMEM((queries, rows, cols), f32),
            pltpu.VMEM((rows * queries, 2 * cols), bf16),
            pltpu.SMEM((rows,), jnp.int32),
            pltpu.VMEM((2, width), jnp.int32),
            pltpu.VMEM((depth, span), f32),
            pltpu.VMEM((trains, span), f32),
            pltpu.VMEM((depth, span), bf16),
            pltpu.VMEM((depth, span), bf16),
            pltpu.VMEM((trains, span), bf16),
            pltpu.VMEM((trains, span), bf16),
            pltpu.VMEM((n_narrow, n_wide) + unit, f32),
            pltpu.VMEM((2, n_wide) + unit, f32),
            pltpu.VMEM((n_wide,) + unit, f32),
            pltpu.VMEM((n_wide,) + unit, f32),
            pltpu.VMEM((n_wide,) + unit, f32),
            pltpu.VMEM((n_wide - 1,) + unit, f32),
            pltpu.VMEM((n_narrow,) + unit, f32),
            pltpu.VMEM((n_wide,) + unit, f32),
            pltpu.VMEM((n_wide - 1,) + unit, f32),
            pltpu.VMEM((n_wide,) + unit, f32),
            pltpu.VMEM((n_narrow, mine_rows, trains), f32),
            pltpu.VMEM((n_narrow - 1, mine_rows, trains), f32),
            pltpu.VMEM((mine_rows, 128), f32),
            pltpu.VMEM((n_narrow - 1, mine_rows, 128), f32),
            pltpu.VMEM((mine_rows, 128), f32),
            pltpu.VMEM((n_wide - 1, mine_rows, 128), f32),
            pltpu.SemaphoreType.DMA((5,)),
            *sems(2),
            *sems(n_wide),
            *sems(n_wide - 1),
            *sems(n_narrow - 1),
            *sems(n_wide - 1),
            *sems(n_wide - 1),
            *sems(n_narrow - 1),
            *sems(n_narrow - 1),
            *sems(n_wide - 1),
        ],
        compiler_params=pltpu.CompilerParams(
            collective_id=0, has_side_effects=True, vmem_limit_bytes=63 * 1024 * 1024
        ),
    )(gradients, offsets, seeds, inv_kernel, sketches)


def solution(mesh):
    placed = (P(None, "narrow", "wide"), P("narrow"), P(), P("wide", "narrow"), P("wide", "narrow"))
    n_wide, n_narrow = mesh.shape["wide"], mesh.shape["narrow"]

    def local(gradients, offsets, seeds, inv_kernel, sketches):
        queries, rows, cols = gradients.shape
        fits = (
            seeds.shape[1] == n_wide * n_narrow * 128
            and n_narrow == 4
            and n_wide % 2 == 0
            and cols == 128
            and rows <= 8
            and queries % (8 * n_narrow) == 0
            and sketches.shape[0] == 128
        )
        if fits:
            return fused(n_wide, n_narrow, gradients, offsets, seeds, inv_kernel, sketches)
        return body(gradients, offsets, seeds, inv_kernel, sketches)

    return jax.shard_map(
        local, mesh=mesh, in_specs=placed, out_specs=P("narrow", "wide"), check_vma=False
    )
```

```python
import functools
import math

import jax
import jax.numpy as jnp
from jax import lax
from jax.experimental import pallas as pl
from jax.experimental.pallas import tpu as pltpu
from jax.sharding import PartitionSpec as P

modulus = 8191
turn = 2.0 * math.pi / 8191.0
epsilon = 1e-06


def cosine_block(param_index, mults, adds):
    phase = (
        (param_index % modulus)[:, None] * (mults % modulus)[None, :] + adds[None, :]
    ) % modulus
    return jnp.cos(phase.astype(jnp.float32) * turn).astype(jnp.bfloat16)


def body(gradients, offsets, seeds, inv_kernel, sketches):
    queries = gradients.shape[0]
    cols_dev = gradients.shape[2]
    flat_grad = gradients.reshape(queries, -1)
    width = seeds.shape[1]
    n_wide = lax.axis_size("wide")
    n_narrow = lax.axis_size("narrow")
    param_index = (
        offsets[:, None]
        + lax.axis_index("wide") * cols_dev
        + jnp.arange(cols_dev, dtype=jnp.int32)[None, :]
    ).reshape(-1)
    local_squares = jnp.sum(jnp.square(flat_grad.astype(jnp.float32)), axis=1)
    start = jnp.int32(0)
    step = min(lax.axis_size("wide") * (width // n_wide), 512)
    pieces = []
    for block_id in range(lax.axis_size("wide") * (width // n_wide) // step):
        begin = start + block_id * step
        mults = lax.dynamic_slice_in_dim(seeds[0], begin, step)
        adds = lax.dynamic_slice_in_dim(seeds[1], begin, step)
        table = cosine_block(param_index, mults, adds)
        term = jnp.einsum("pk,qp->kq", table, flat_grad, preferred_element_type=jnp.float32)
        pieces.append(term)
    owned = lax.psum_scatter(
        jnp.concatenate(pieces, axis=0), "wide", scatter_dimension=0, tiled=True
    )
    owned = lax.psum(owned, "narrow")
    kernel_part = lax.dot_general(
        owned,
        inv_kernel,
        (((0,), (0,)), ((), ())),
        precision=lax.Precision.HIGHEST,
        preferred_element_type=jnp.float32,
    )
    preconditioned = lax.psum(kernel_part, "wide")
    rows = queries // n_narrow
    root = jnp.sqrt(jnp.float32(width))
    product = lax.dot_general(
        preconditioned,
        sketches,
        (((1,), (1,)), ((), ())),
        precision=lax.Precision.HIGHEST,
        preferred_element_type=jnp.float32,
    )
    scores = lax.psum_scatter(product / root, "narrow", scatter_dimension=0, tiled=True)
    total = lax.psum(local_squares, ("wide", "narrow"))
    late_scale = 1.0 / jnp.sqrt(total + epsilon)
    mine = lax.dynamic_slice_in_dim(late_scale, lax.axis_index("narrow") * rows, rows)
    scores = scores * mine[:, None]
    return scores


def split(value):
    high = value.astype(jnp.bfloat16)
    low = (value - high.astype(jnp.float32)).astype(jnp.bfloat16)
    return high, low


def fold(value):
    return (value & modulus) + (value >> 13)


def cos_sin(phase):
    centred = jnp.where(phase > modulus // 2, phase - modulus, phase)
    half = centred.astype(jnp.float32) * jnp.float32(math.pi / modulus)
    square = half * half
    sine = jnp.full_like(square, -1.0 / math.factorial(11))
    for power in (9, 7, 5, 3, 1):
        sine = sine * square + jnp.float32((-1.0) ** (power // 2) / math.factorial(power))
    sine = sine * half
    cosine = jnp.full_like(square, 1.0 / math.factorial(12))
    for power in (10, 8, 6, 4, 2, 0):
        cosine = cosine * square + jnp.float32((-1.0) ** (power // 2) / math.factorial(power))
    return 1.0 - 2.0 * sine * sine, 2.0 * sine * cosine


def kernel(
    n_wide, n_narrow, grads_hbm, offsets_hbm, seeds_hbm, inv_hbm, sketch_hbm, out_ref,
    grads_in, grads_f32, grads_ref, offsets_ref, seeds_ref, inv_f32, sketch_f32, inv_hi, inv_lo, sketch_hi, sketch_lo,
    part, from_core, to_x, from_x, mine, from_wide, owned,
    product, from_wide2, full, scored, from_narrow,
    sq_mine, sq_narrow, sq_sum, sq_wide,
    local_sem, core_send, core_recv, x_send, x_recv, wide_send, wide_recv,
    gather_send, gather_recv, wide2_send, wide2_recv, full_send, full_recv,
    last_send, last_recv, sqn_send, sqn_recv, sqw_send, sqw_recv,
):
    w = lax.axis_index("wide")
    n = lax.axis_index("narrow")
    sibling = n + 1 - 2 * lax.rem(n, 2)
    across = lax.rem(n + 2, n_narrow)
    diagonal = lax.rem(sibling + 2, n_narrow)
    width = seeds_ref.shape[1]
    block = width // n_wide
    rows = offsets_ref.shape[0]
    queries, _, cols = grads_in.shape

    def wide_peer(s):
        return lax.rem(w + s, n_wide)

    def narrow_peer(s):
        return lax.rem(n + s, n_narrow)

    def remote(src, dst, send, recv, to_wide, to_narrow):
        return pltpu.make_async_remote_copy(
            src_ref=src, dst_ref=dst, send_sem=send, recv_sem=recv,
            device_id=(to_wide, to_narrow), device_id_type=pl.DeviceIdType.MESH,
        )

    load_inv = pltpu.make_async_copy(inv_hbm, inv_f32, local_sem.at[0])
    load_sketch = pltpu.make_async_copy(sketch_hbm, sketch_f32, local_sem.at[1])
    load_grads = pltpu.make_async_copy(grads_hbm, grads_in, local_sem.at[2])
    load_seeds = pltpu.make_async_copy(seeds_hbm, seeds_ref, local_sem.at[3])
    load_offsets = pltpu.make_async_copy(offsets_hbm, offsets_ref, local_sem.at[4])
    load_grads.start()
    load_seeds.start()
    load_offsets.start()
    load_inv.start()
    load_sketch.start()

    barrier = pltpu.get_barrier_semaphore()
    for s in range(1, n_wide):
        pl.semaphore_signal(barrier, inc=1, device_id=(wide_peer(s), n), device_id_type=pl.DeviceIdType.MESH)
    for s in range(1, n_narrow):
        pl.semaphore_signal(barrier, inc=1, device_id=(w, narrow_peer(s)), device_id_type=pl.DeviceIdType.MESH)

    load_grads.wait()
    grads_f32[...] = grads_in[...].astype(jnp.float32)
    by_query = jnp.zeros((queries, cols), jnp.float32)
    for r in range(rows):
        one_row = grads_f32[:, r, :]
        by_query = by_query + jnp.square(one_row)
        one_row = one_row.astype(jnp.bfloat16)
        grads_ref[r * queries : (r + 1) * queries, :cols] = one_row
        grads_ref[r * queries : (r + 1) * queries, cols:] = one_row
    by_query = jnp.broadcast_to(jnp.sum(by_query, axis=1, keepdims=True), (queries, 128))
    mine_rows = queries // n_narrow
    group = lax.broadcasted_iota(jnp.int32, (mine_rows, 128), 1) // (128 // n_narrow)
    tile = by_query[:mine_rows]
    for j in range(1, n_narrow):
        tile = jnp.where(group == j, by_query[j * mine_rows : (j + 1) * mine_rows], tile)
    sq_mine[...] = tile

    load_offsets.wait()
    load_seeds.wait()
    bases = [fold(offsets_ref[r] + w * cols) for r in range(rows)]
    steps = cols // 16

    def project(slab):
        def chunk(j, carry):
            units = []
            for half in range(2):
                start = pl.multiple_of((2 * j + half) * block + slab * 128, 128)
                units.append(seeds_ref[:, pl.ds(start, 128)])
            seeds = jnp.concatenate(units, axis=1)
            mult = fold(seeds[0:1])
            add = seeds[1:2]
            at = lax.broadcasted_iota(jnp.int32, (steps + 16, 256), 0)
            factor = jnp.where(at < steps, at * 16, at - steps)
            col_cos, col_sin = cos_sin(fold(fold(factor * mult)))
            at = lax.broadcasted_iota(jnp.int32, (8, 256), 0)
            base = jnp.full((8, 256), bases[0], jnp.int32)
            for r in range(1, rows):
                base = jnp.where(at == r, bases[r], base)
            row_cos, row_sin = cos_sin(fold(fold(base * mult + add)))
            low_cos, low_sin = col_cos[steps:], col_sin[steps:]
            cos_parts, sin_parts = [], []
            for h in range(steps):
                high_cos, high_sin = col_cos[h : h + 1], col_sin[h : h + 1]
                cos_parts.append(split(high_cos * low_cos - high_sin * low_sin))
                sin_parts.append(split(high_sin * low_cos + high_cos * low_sin))
            cos_table = jnp.concatenate([p[0] for p in cos_parts] + [p[1] for p in cos_parts], axis=0)
            sin_table = jnp.concatenate([p[0] for p in sin_parts] + [p[1] for p in sin_parts], axis=0)
            by_cos = jnp.dot(grads_ref[...], cos_table, preferred_element_type=jnp.float32)
            by_sin = jnp.dot(grads_ref[...], sin_table, preferred_element_type=jnp.float32)
            total = jnp.zeros((queries, 256), jnp.float32)
            for r in range(rows):
                here = slice(r * queries, (r + 1) * queries)
                total = total + (row_cos[r : r + 1] * by_cos[here] - row_sin[r : r + 1] * by_sin[here])
            part[slab, 2 * j] = total[:, :128]
            part[slab, 2 * j + 1] = total[:, 128:]
            return carry

        lax.fori_loop(0, n_wide // 2, chunk, 0)

    project(diagonal)
    pl.semaphore_wait(barrier, n_wide + n_narrow - 2)
    core_copies = []
    copy = remote(part.at[diagonal], from_core.at[0], core_send.at[0], core_recv.at[0], w, sibling)
    copy.start()
    core_copies.append(copy)
    sqn_copies = []
    for s in range(1, n_narrow):
        copy = remote(sq_mine, sq_narrow.at[s - 1], sqn_send.at[s - 1], sqn_recv.at[s - 1], w, narrow_peer(s))
        copy.start()
        sqn_copies.append(copy)
    project(across)
    core_copies[0].wait_recv()
    order = [*range(1, n_wide), 0]
    x_copies = []
    for s in order:
        at = wide_peer(s)
        to_x[at] = part[across, at] + from_core[0, at]
        copy = remote(to_x.at[at], from_x.at[at], x_send.at[s], x_recv.at[s], w, across)
        copy.start()
        x_copies.append(copy)
    project(sibling)
    copy = remote(part.at[sibling], from_core.at[1], core_send.at[1], core_recv.at[1], w, sibling)
    copy.start()
    core_copies.append(copy)
    project(n)
    core_copies[1].wait_recv()
    wide_copies = []
    for s, x_copy in zip(order, x_copies):
        at = wide_peer(s)
        x_copy.wait_recv()
        mine[at] = part[n, at] + from_core[1, at] + from_x[at]
        if s:
            copy = remote(mine.at[at], from_wide.at[s - 1], wide_send.at[s - 1], wide_recv.at[s - 1], at, n)
            copy.start()
            wide_copies.append(copy)
    for copy in sqn_copies:
        copy.wait_recv()
    total = sq_mine[...]
    for s in range(1, n_narrow):
        total = total + sq_narrow[s - 1]
    sq_sum[...] = total
    sqw_copies = []
    for s in range(1, n_wide):
        copy = remote(sq_sum, sq_wide.at[s - 1], sqw_send.at[s - 1], sqw_recv.at[s - 1], wide_peer(s), n)
        copy.start()
        sqw_copies.append(copy)
    load_inv.wait()
    load_sketch.wait()
    slab_rows = 32

    def split_inv(i, carry):
        at = pl.ds(pl.multiple_of(i * slab_rows, slab_rows), slab_rows)
        inv_hi[at, :], inv_lo[at, :] = split(inv_f32[at, :])
        return carry

    def split_sketch(i, carry):
        at = pl.ds(pl.multiple_of(i * slab_rows, slab_rows), slab_rows)
        sketch_hi[at, :], sketch_lo[at, :] = split(sketch_f32[at, :])
        return carry

    lax.fori_loop(0, inv_f32.shape[0] // slab_rows, split_inv, 0)
    lax.fori_loop(0, sketch_f32.shape[0] // slab_rows, split_sketch, 0)

    total = mine[w]
    for s in range(1, n_wide):
        wide_copies[s - 1].wait_recv()
        total = total + from_wide[s - 1]
    owned[n] = total
    gather_copies = []
    for s in range(1, n_narrow):
        copy = remote(owned.at[n], owned.at[n], gather_send.at[s - 1], gather_recv.at[s - 1], w, narrow_peer(s))
        copy.start()
        gather_copies.append(copy)
    for copy in gather_copies:
        copy.wait_recv()
    high, low = split(jnp.concatenate([owned[i] for i in range(n_narrow)], axis=1))
    both = jnp.dot(jnp.concatenate([high, low], axis=0), inv_hi[...], preferred_element_type=jnp.float32)
    both = both[:queries] + both[queries:] + jnp.dot(high, inv_lo[...], preferred_element_type=jnp.float32)
    for i in range(n_wide):
        product[i] = both[:, i * 128 : (i + 1) * 128]
    wide2_copies = []
    for s in range(1, n_wide):
        at = wide_peer(s)
        copy = remote(product.at[at], from_wide2.at[s - 1], wide2_send.at[s - 1], wide2_recv.at[s - 1], at, n)
        copy.start()
        wide2_copies.append(copy)
    total = sq_sum[...]
    for s in range(1, n_wide):
        sqw_copies[s - 1].wait_recv()
        total = total + sq_wide[s - 1]
    own_squares = jnp.max(jnp.where(group == n, total, 0.0), axis=1, keepdims=True)
    scale = 1.0 / jnp.sqrt(own_squares + epsilon)
    scale = scale * jnp.float32(1.0 / math.sqrt(width))

    total = product[w]
    for s in range(1, n_wide):
        wide2_copies[s - 1].wait_recv()
        total = total + from_wide2[s - 1]
    full[w] = total
    full_copies = []
    for s in range(1, n_wide):
        copy = remote(full.at[w], full.at[w], full_send.at[s - 1], full_recv.at[s - 1], wide_peer(s), n)
        copy.start()
        full_copies.append(copy)
    for copy in full_copies:
        copy.wait_recv()
    high, low = split(jnp.concatenate([full[i] for i in range(n_wide)], axis=1))
    last = (((1,), (1,)), ((), ()))
    both = lax.dot_general(jnp.concatenate([high, low], axis=0), sketch_hi[...], last, preferred_element_type=jnp.float32)
    both = both[:queries] + both[queries:] + lax.dot_general(
        high, sketch_lo[...], last, preferred_element_type=jnp.float32
    )
    for i in range(n_narrow):
        scored[i] = both[i * mine_rows : (i + 1) * mine_rows]
    last_copies = []
    for s in range(1, n_narrow):
        at = narrow_peer(s)
        copy = remote(scored.at[at], from_narrow.at[s - 1], last_send.at[s - 1], last_recv.at[s - 1], w, at)
        copy.start()
        last_copies.append(copy)
    total = scored[n]
    for s in range(1, n_narrow):
        last_copies[s - 1].wait_recv()
        total = total + from_narrow[s - 1]
    out_ref[...] = total * scale
    for group_copies in (
        core_copies, x_copies, wide_copies, sqn_copies, sqw_copies, gather_copies, wide2_copies, full_copies, last_copies,
    ):
        for copy in group_copies:
            copy.wait_send()


def fused(n_wide, n_narrow, gradients, offsets, seeds, inv_kernel, sketches):
    queries, rows, cols = gradients.shape
    width = seeds.shape[1]
    depth, span = inv_kernel.shape
    trains = sketches.shape[0]
    unit = (queries, 128)
    mine_rows = queries // n_narrow
    f32, bf16 = jnp.float32, jnp.bfloat16

    def sems(count):
        return [pltpu.SemaphoreType.DMA((count,))] * 2

    return pl.pallas_call(
        functools.partial(kernel, n_wide, n_narrow),
        out_shape=jax.ShapeDtypeStruct((mine_rows, trains), f32),
        in_specs=[pl.BlockSpec(memory_space=pltpu.HBM)] * 5,
        out_specs=pl.BlockSpec(memory_space=pltpu.VMEM),
        scratch_shapes=[
            pltpu.VMEM((queries, rows, cols), bf16),
            pltpu.VMEM((queries, rows, cols), f32),
            pltpu.VMEM((rows * queries, 2 * cols), bf16),
            pltpu.SMEM((rows,), jnp.int32),
            pltpu.VMEM((2, width), jnp.int32),
            pltpu.VMEM((depth, span), f32),
            pltpu.VMEM((trains, span), f32),
            pltpu.VMEM((depth, span), bf16),
            pltpu.VMEM((depth, span), bf16),
            pltpu.VMEM((trains, span), bf16),
            pltpu.VMEM((trains, span), bf16),
            pltpu.VMEM((n_narrow, n_wide) + unit, f32),
            pltpu.VMEM((2, n_wide) + unit, f32),
            pltpu.VMEM((n_wide,) + unit, f32),
            pltpu.VMEM((n_wide,) + unit, f32),
            pltpu.VMEM((n_wide,) + unit, f32),
            pltpu.VMEM((n_wide - 1,) + unit, f32),
            pltpu.VMEM((n_narrow,) + unit, f32),
            pltpu.VMEM((n_wide,) + unit, f32),
            pltpu.VMEM((n_wide - 1,) + unit, f32),
            pltpu.VMEM((n_wide,) + unit, f32),
            pltpu.VMEM((n_narrow, mine_rows, trains), f32),
            pltpu.VMEM((n_narrow - 1, mine_rows, trains), f32),
            pltpu.VMEM((mine_rows, 128), f32),
            pltpu.VMEM((n_narrow - 1, mine_rows, 128), f32),
            pltpu.VMEM((mine_rows, 128), f32),
            pltpu.VMEM((n_wide - 1, mine_rows, 128), f32),
            pltpu.SemaphoreType.DMA((5,)),
            *sems(2),
            *sems(n_wide),
            *sems(n_wide - 1),
            *sems(n_narrow - 1),
            *sems(n_wide - 1),
            *sems(n_wide - 1),
            *sems(n_narrow - 1),
            *sems(n_narrow - 1),
            *sems(n_wide - 1),
        ],
        compiler_params=pltpu.CompilerParams(
            collective_id=0, has_side_effects=True, vmem_limit_bytes=63 * 1024 * 1024
        ),
    )(gradients, offsets, seeds, inv_kernel, sketches)


def solution(mesh):
    placed = (P(None, "narrow", "wide"), P("narrow"), P(), P("wide", "narrow"), P("wide", "narrow"))
    n_wide, n_narrow = mesh.shape["wide"], mesh.shape["narrow"]

    def local(gradients, offsets, seeds, inv_kernel, sketches):
        queries, rows, cols = gradients.shape
        fits = (
            seeds.shape[1] == n_wide * n_narrow * 128
            and n_narrow == 4
            and n_wide % 2 == 0
            and cols == 128
            and rows <= 8
            and queries % (8 * n_narrow) == 0
            and sketches.shape[0] == 128
        )
        if fits:
            return fused(n_wide, n_narrow, gradients, offsets, seeds, inv_kernel, sketches)
        return body(gradients, offsets, seeds, inv_kernel, sketches)

    return jax.shard_map(
        local, mesh=mesh, in_specs=placed, out_specs=P("narrow", "wide"), check_vma=False
    )
```
